32 devices in a mesh: sec: 2 (over core), gx: 4 (over y, x), gy: 4 (over z).
Axes of the slice: x: 2, y: 2, z: 4, core: 2. Of those that a mesh axis runs over, the one named last changes fastest.
Arguments:
- adjoint_state: float32 [2, 10, 512, 512], P('sec', None, 'gx', 'gy'), may hold values from -6 to 6
- forcing: float32 [2, 10, 512, 512], P('sec', None, 'gx', 'gy'), may hold values from -6 to 6
- viscosity: float32 [2, 512, 512], P('sec', 'gx', 'gy'), may hold values from 0.5 to 4
- reaction: float32 [2, 512, 512], P('sec', 'gx', 'gy'), may hold values from 0.1 to 1
- source_patch: int32 [2, 2048], P('sec', ('gx', 'gy')), may hold values from 0 to 63
- owner: int32 [2, 2048, 1], P('sec', ('gx', 'gy')), may hold values from 0 to 15; in each aligned block of 128 rows (0 to 127, 128 to 255, ..., all dimensions but the last counted through in order) at most 16 rows name the same one
- cavity_map: int32 [2, 16, 16, 16], P('sec', ('gx', 'gy')), may hold values from 0 to 63
Outputs:
- adjoint_field: float32 [2, 10, 512, 512], P('sec', None, 'gx', 'gy')
The draws below stay inside these ranges and needn't reach their ends.
Inputs may be any that keep to these rules, and one draw needn't show every extreme that they name: The entries of one device name each owner at most 16 times, a bound that some block reaches.
All inputs are finite; a program needn't handle non-finite values.
Results may differ from the reference program's by a relative error of at most 0.00002.
Values sent between devices are 32-bit elements; how exact they have to be, the bound alone decides.
A program may use at most 64 MiB of HBM per device.

```python
import math
import jax
import jax.numpy as jnp
import numpy as np

LEV = 10
CX = 128
CY = 128
PATCH = 2
PW = 128
SWEEPS = 8
TPD = 128
GRID_DEV = 16
CAP = 16
NPATCH = 64
NX = 512
NY = 512
N_GX = 4
N_GY = 4


def place_ends(values, key, low, high):
    dims = values.shape
    spot = [jax.random.randint(jax.random.fold_in(key, axis), (), 0, dims[axis]) for axis in range(len(dims))]
    values = values.at[tuple(spot)].set(low)
    longest = dims.index(max(dims))
    spot[longest] = (spot[longest] + 1) % dims[longest]
    return values.at[tuple(spot)].set(high)


def level_of(rng, dims, cuts, low, top_value):
    level = 1.0
    for dim, shards_of in cuts:
        steps = jax.random.uniform(jax.random.fold_in(jax.random.fold_in(rng, 6), dim), (shards_of,), jnp.float32, low / len(cuts), top_value / len(cuts))
        level = level * jnp.repeat(jnp.exp(steps), dims[dim] // shards_of).reshape((-1,) + (1,) * (len(dims) - 1 - dim))
    return level


def assign_block(rng, own, number, rows, number_of, top, reach, skew):
    ranking = jax.random.permutation(rng, number_of)
    packed, usual = load_shares(number_of, rows * top, reach, skew, True), load_shares(number_of, rows * top, reach, skew, False)
    places = jnp.arange(number_of)

    def named(lengths, rotation):
        used = int((lengths > 0).sum())
        fixed = max(1, used // 4)
        passed = fixed + (places - fixed + rotation * (used - fixed)) % max(1, number_of - fixed)
        return jnp.zeros((number_of,), jnp.int32).at[ranking[jnp.where(places < fixed, places, passed)]].set(jnp.asarray(lengths, jnp.int32))

    lengths = jnp.where(number % 4 == 0, named(packed, number // 4), named(usual, number - number // 4 - 1))
    mixed = jax.random.permutation(jax.random.fold_in(own, 3), number_of)
    giver, taker = mixed[0:number_of // 2 * 2:2], mixed[1:number_of // 2 * 2:2]
    room = jnp.minimum(lengths[giver] - 1, reach - lengths[taker]) // 2
    room = jnp.where((giver == ranking[0]) | (taker == ranking[0]) | (lengths[taker] == 0), 0, jnp.maximum(room, 0))
    passed = jax.random.randint(jax.random.fold_in(own, 4), (number_of // 2,), 0, 1 << 20) % (room + 1)
    lengths = lengths.at[giver].add(-passed).at[taker].add(passed)
    items = jnp.searchsorted(jnp.cumsum(lengths), jnp.arange(rows * top), side="right").astype(jnp.int32)
    table = items.reshape(top, rows).T
    table = table[jax.random.permutation(jax.random.fold_in(own, 1), rows)]
    rotation = jax.random.randint(jax.random.fold_in(own, 2), (rows, 1), 0, top)
    return jnp.take_along_axis(table, (jnp.arange(top)[None, :] + rotation) % top, axis=1)


def load_shares(count, total, most, skew, full):
    loads = [(1 << 20) // math.isqrt(rank ** skew) + 1 for rank in range(1, count + 1)]
    largest = most if full else min(most, max(-(-total // count), total * loads[0] // sum(loads)))
    least = 1 if total - largest >= count - 1 else 0
    counts, rest = [largest] + [least] * (count - 1), total - largest - least * (count - 1)
    while rest > 0:
        free = [i for i in range(1, count) if counts[i] < largest] or [i for i in range(1, count) if counts[i] < most]
        mass, budget = sum([loads[i] for i in free]), rest
        for i in free:
            more = min(most - counts[i], max(1, budget * loads[i] // mass), rest)
            counts[i] = counts[i] + more
            rest = rest - more
    return np.array(counts)


def noise(rng, dims, scale, most, cuts=(), held_as=jnp.bfloat16):
    array = scale * jax.random.normal(rng, dims, jnp.float32)
    if cuts:
        array = array * level_of(rng, dims, cuts, -0.22, 0.18)
    return jnp.clip(array, -most, most).astype(held_as)


def setup_inputs(seed: int = 0) -> dict:
    seeds = jax.random.split(jax.random.key(seed), 8)
    adjoint_state = noise(seeds[0], (2, LEV, NX, NY), 1.0, 6.0, ((0, 2), (2, 4), (3, 4)), jnp.float32)
    forcing = noise(seeds[1], (2, LEV, NX, NY), 1.0, 6.0, ((0, 2), (2, 4), (3, 4)), jnp.float32)
    viscosity = jnp.clip(jnp.exp(math.log(4.0) - 2.0794415 * jax.random.uniform(seeds[2], (2, NX, NY), jnp.float32) ** level_of(seeds[2], (2, NX, NY), ((0, 2), (1, 4), (2, 4)), -0.2, 0.2)), 0.5, 4.0)
    reaction = jnp.clip(jnp.exp(math.log(1.0) - 2.3025851 * jax.random.uniform(seeds[3], (2, NX, NY), jnp.float32) ** level_of(seeds[3], (2, NX, NY), ((0, 2), (1, 4), (2, 4)), -0.2, 0.2)), 0.1, 1.0)
    source_patch = place_ends(jax.random.randint(seeds[4], (2, GRID_DEV * TPD), 0, NPATCH), jax.random.fold_in(seeds[4], 1), 0, NPATCH - 1).astype(jnp.int32)
    owner_keys = jax.random.split(jax.random.fold_in(seeds[5], 1), 2 * (GRID_DEV * TPD) // TPD)
    owner_turns = jax.random.permutation(jax.random.fold_in(seeds[5], 3), 2 * (GRID_DEV * TPD) // TPD)
    owner = jax.vmap(lambda own, number: assign_block(jax.random.fold_in(seeds[5], 2), own, number, TPD, GRID_DEV, 1, CAP, 2))(owner_keys, owner_turns).reshape((2, GRID_DEV * TPD, 1))
    cavity_map = place_ends(jax.random.randint(seeds[6], (2, GRID_DEV, GRID_DEV, CAP), 0, NPATCH), jax.random.fold_in(seeds[6], 1), 0, NPATCH - 1).astype(jnp.int32)
    return {"adjoint_state": adjoint_state, "forcing": forcing, "viscosity": viscosity, "reaction": reaction, "source_patch": source_patch, "owner": owner, "cavity_map": cavity_map}


OMEGA = 0.8
KAPPA = 0.5


def relax_all(field, visc, invd, force):
    padded = jnp.pad(field, ((0, 0), (0, 0), (1, 1), (1, 1)))
    beside = padded[:, :, 2:, 1:-1] + padded[:, :, :-2, 1:-1]
    beside = beside + padded[:, :, 1:-1, 2:] + padded[:, :, 1:-1, :-2]
    return (1.0 - OMEGA) * field + OMEGA * invd * (force + visc * beside)


def reference(adjoint_state, forcing, viscosity, reaction, source_patch, owner, cavity_map):
    groups = N_GX * N_GY
    invd = (1.0 / (4.0 * viscosity + reaction))[:, None]
    visc = viscosity[:, None]
    field = adjoint_state
    for step in range(SWEEPS // 2):
        field = relax_all(field, visc, invd, forcing)
    blocks = field.reshape(2, LEV, N_GX, CX // PATCH, PATCH, N_GY, CY // PW, PW)
    patches = blocks.transpose(0, 2, 5, 3, 6, 1, 4, 7).reshape(2, groups, NPATCH, LEV, PATCH, PW)
    srcs = source_patch.reshape(2, groups, TPD)
    dests = owner.reshape(2, groups, TPD)
    sidx = jnp.broadcast_to(jnp.arange(2, dtype=jnp.int32)[:, None, None], srcs.shape)
    gidx = jnp.broadcast_to(jnp.arange(groups, dtype=jnp.int32)[None, :, None], srcs.shape)
    oidx = 1 - sidx
    onehot = (dests[..., None] == jnp.arange(groups, dtype=jnp.int32)).astype(jnp.int32)
    before = jnp.cumsum(onehot, axis=2) - onehot
    rank = jnp.sum(before * onehot, axis=3).astype(jnp.int32)
    recv = cavity_map[oidx, dests, gidx, rank]
    sent = patches[sidx, gidx, srcs]
    local = patches[oidx, dests, recv]
    updated = patches.at[oidx, dests, recv].add(KAPPA * sent)
    updated = updated.at[sidx, gidx, srcs].add(local * jnp.tanh(sent))
    blocks = updated.reshape(2, N_GX, N_GY, CX // PATCH, CY // PW, LEV, PATCH, PW)
    field = blocks.transpose(0, 5, 1, 3, 6, 2, 4, 7).reshape(2, LEV, N_GX * CX, N_GY * CY)
    for step in range(SWEEPS // 2):
        field = relax_all(field, visc, invd, forcing)
    return field
```

```python
import functools

import jax
import jax.numpy as jnp
from jax import lax
from jax.experimental import pallas as pl
from jax.experimental.pallas import tpu as pltpu
from jax.sharding import PartitionSpec as P

OMEGA = 0.8
KAPPA = 0.5
HALF = 4
EDGE = 8
LANES = 128
MESH = pl.DeviceIdType.MESH
BF16 = jnp.bfloat16
F32 = jnp.float32


def iota(shape, dim):
    return lax.broadcasted_iota(jnp.int32, shape, dim)


def kernel(
    n_gx, n_gy, groups, cap, levels, chunk,
    x_ref, f_ref, v_ref, r_ref, src_ref, own_ref, map_ref, out_ref,
    xe, fe, be, rs1, rr1, ps1, pr1, rs2, rr2, ps2, pr2,
    tz, tp, weights, pieces, gz, parts, arrived,
    halo_send, halo_recv, tz_send, tz_recv, tp_send, tp_recv,
    z_send, z_recv, p_send, p_recv,
):
    sec, gx, gy = lax.axis_index("sec"), lax.axis_index("gx"), lax.axis_index("gy")
    rows = x_ref.shape[2]
    tall = rows + 2 * EDGE
    chunks = levels // chunk
    has = {-1: gx > 0, 0: True, 1: gx < n_gx - 1}
    has_y = {-1: gy > 0, 0: True, 1: gy < n_gy - 1}
    around = [(a, b) for a in (-1, 0, 1) for b in (-1, 0, 1) if (a, b) != (0, 0)]

    def exists(a, b):
        if a == 0:
            return has_y[b]
        if b == 0:
            return has[a]
        return jnp.logical_and(has[a], has_y[b])

    lane = iota((LANES, LANES), 1)
    row = iota((LANES, LANES), 0)
    named = jnp.where(own_ref[0] == lane, 1.0, 0.0).astype(BF16)
    earlier = jnp.where(lane < row, 1.0, 0.0).astype(BF16)
    before = jnp.dot(earlier, named, preferred_element_type=F32)
    rank = jnp.sum(before * named.astype(F32), axis=1, keepdims=True)
    source = jnp.sum(
        jnp.where(lane == row, src_ref[...].astype(F32) + 1.0, 0.0), axis=1, keepdims=True
    )
    ranked = jnp.where(rank == lane.astype(F32), source, 0.0).astype(BF16)
    slots = lax.dot_general(
        named, ranked, (((0,), (0,)), ((), ())), preferred_element_type=F32
    )
    tz[gy, 0:groups] = slots[0:groups]
    tz[gy, groups : 2 * groups] = jnp.full((groups, LANES), -1.0, F32)
    tz[gy, groups : 2 * groups, 0:cap] = map_ref[0, 0].astype(F32)

    inv = OMEGA / (4.0 * v_ref[0] + r_ref[0])
    be[...] = jnp.zeros_like(be)
    be[EDGE : EDGE + rows, 0:LANES] = inv * v_ref[0]
    for l in range(levels):
        fe[l, EDGE : EDGE + rows, 0:LANES] = inv * f_ref[0, l]

    def pack(planes, rs, ps):
        small = iota((rows, LANES), 1)
        for first in range(0, len(planes), 16):
            packed = jnp.zeros((rows, LANES), F32)
            for k, read in enumerate(planes[first : first + 16]):
                tile = read()
                rs[0, first + k] = tile[0:EDGE]
                rs[1, first + k] = tile[rows - EDGE : rows]
                low = tile if k == 0 else pltpu.roll(tile, 8 * k, 1)
                high = tile if k == 15 else pltpu.roll(tile, 8 * k + 8, 1)
                packed = jnp.where(small // 4 == 2 * k, low, packed)
                packed = jnp.where(small // 4 == 2 * k + 1, high, packed)
            ps[first // 16] = packed

    def halo_copy(phase, a, b, rs, rr, ps, pr):
        if b == 0:
            src, dst = rs.at[(a + 1) // 2], rr.at[(1 - a) // 2]
        else:
            side = (1 - b) // 2
            if a == 0:
                src, dst = ps, pr.at[side, :, EDGE : EDGE + rows]
            elif a == 1:
                src, dst = ps.at[:, rows - EDGE : rows], pr.at[side, :, 0:EDGE]
            else:
                src, dst = ps.at[:, 0:EDGE], pr.at[side, :, EDGE + rows : tall]
        k = around.index((a, b))
        return pltpu.make_async_remote_copy(
            src_ref=src, dst_ref=dst,
            send_sem=halo_send.at[phase, k], recv_sem=halo_recv.at[phase, k],
            device_id=(sec, gx + a, gy + b), device_id_type=MESH,
        )

    def halo_start(phase, *refs):
        for a, b in around:
            @pl.when(exists(a, b))
            def _():
                halo_copy(phase, a, b, *refs).start()

    def halo_wait(phase, rs, rr, ps, pr):
        for a, b in around:
            @pl.when(exists(-a, -b))
            def _():
                halo_copy(phase, a, b, rs, rr, ps, pr).wait_recv()

            @pl.when(exists(a, b))
            def _():
                halo_copy(phase, a, b, rs, rr, ps, pr).wait_send()

    def beside(pr, k):
        small = iota((tall, LANES), 1)
        at = 8 * (k % 16)
        right, left = pr[1, k // 16], pr[0, k // 16]
        right = right if at == 0 else pltpu.roll(right, LANES - at, 1)
        left = left if at == 120 else pltpu.roll(left, 120 - at, 1)
        return jnp.where(small < HALF, right, jnp.where(small >= LANES - HALF, left, 0.0))

    def sweeps(l):
        field, push, pull = xe[l], fe[l], be[...]
        for _ in range(HALF):
            near = pltpu.roll(field, 1, 0) + pltpu.roll(field, tall - 1, 0)
            near = near + pltpu.roll(field, 1, 1) + pltpu.roll(field, 2 * LANES - 1, 1)
            field = (1.0 - OMEGA) * field + push + pull * near
        return field[EDGE : EDGE + rows, 0:LANES]

    planes = [functools.partial(lambda l: x_ref[0, l], l) for l in range(levels)]
    planes += [
        functools.partial(lambda l: fe[l, EDGE : EDGE + rows, 0:LANES], l)
        for l in range(levels)
    ]
    planes += [lambda: be[EDGE : EDGE + rows, 0:LANES]]
    pack(planes, rs1, ps1)
    for ref in (rr1, pr1, rr2, pr2):
        ref[...] = jnp.zeros_like(ref)

    barrier = pltpu.get_barrier_semaphore()

    def hello(*device):
        pl.semaphore_signal(barrier, inc=1, device_id=device, device_id_type=MESH)

    total = n_gx + n_gy - 1
    for k in range(1, n_gy):
        hello(sec, gx, lax.rem(gy + k, n_gy))
    for k in range(n_gx):
        hello(1 - sec, lax.rem(gx + k, n_gx), gy)
    for a, b in around:
        if a != 0:
            there = exists(a, b)
            total = total + jnp.where(there, 1, 0)

            @pl.when(there)
            def _():
                hello(sec, gx + a, gy + b)

    pl.semaphore_wait(barrier, total)

    halo_start(0, rs1, rr1, ps1, pr1)

    def table_z(to, slot):
        return pltpu.make_async_remote_copy(
            src_ref=tz.at[gy], dst_ref=tz.at[slot],
            send_sem=tz_send.at[to], recv_sem=tz_recv.at[slot],
            device_id=(sec, gx, to), device_id_type=MESH,
        )

    def table_p(to, slot):
        return pltpu.make_async_remote_copy(
            src_ref=tz.at[gy], dst_ref=tp.at[slot],
            send_sem=tp_send.at[to], recv_sem=tp_recv.at[slot],
            device_id=(1 - sec, to, gy), device_id_type=MESH,
        )

    def others(act):
        def one(k, _):
            act(lax.rem(gy + k, n_gy))
            return 0
        lax.fori_loop(1, n_gy, one, 0)

    def plane(act):
        def one(k, _):
            act(lax.rem(gx + k, n_gx))
            return 0
        lax.fori_loop(0, n_gx, one, 0)

    others(lambda to: table_z(to, gy).start())
    plane(lambda to: table_p(to, gx).start())

    halo_wait(0, rs1, rr1, ps1, pr1)
    for l in range(levels):
        for ref, k in ((xe, l), (fe, levels + l)):
            ref[l, 0:EDGE, 0:LANES] = rr1[0, k]
            ref[l, EDGE + rows : tall, 0:LANES] = rr1[1, k]
            ref[l, :, LANES : 2 * LANES] = beside(pr1, k)
        xe[l, EDGE : EDGE + rows, 0:LANES] = x_ref[0, l]
    be[0:EDGE, 0:LANES] = rr1[0, 2 * levels]
    be[EDGE + rows : tall, 0:LANES] = rr1[1, 2 * levels]
    be[:, LANES : 2 * LANES] = beside(pr1, 2 * levels)

    def z_copy(c, to, slot):
        return pltpu.make_async_remote_copy(
            src_ref=gz.at[gy, pl.ds(c * chunk, chunk)],
            dst_ref=gz.at[slot, pl.ds(c * chunk, chunk)],
            send_sem=z_send.at[c, to], recv_sem=z_recv.at[c, slot],
            device_id=(sec, gx, to), device_id_type=MESH,
        )

    def first(c, _):
        def one(k, _):
            gz[gy, c * chunk + k] = sweeps(c * chunk + k)
            return 0
        lax.fori_loop(0, chunk, one, 0)
        others(lambda to: z_copy(c, to, gy).start())
        return 0

    lax.fori_loop(0, chunks, first, 0)

    others(lambda at: table_z(at, at).wait_recv())
    plane(lambda at: table_p(at, at).wait_recv())
    patch_row = (row // 2).astype(F32)
    same = (row % 2) == (lane % 2)

    def hot(values):
        return jnp.where(values == patch_row, 1.0, 0.0).astype(BF16)

    def counts(a, b, scale):
        both = lax.dot_general(a, b, (((1,), (1,)), ((), ())), preferred_element_type=F32)
        return jnp.where(same, scale * both, 0.0).astype(BF16)

    def build(d, _):
        dest = d * n_gy + gy
        for z in range(n_gy):
            giver = gx * n_gy + z
            given = hot(tz[z, pl.ds(dest, 1), :] - 1.0)
            taken = hot(tz[z, pl.ds(groups + dest, 1), :])
            asked = hot(tp[d, pl.ds(giver, 1), :] - 1.0)
            put = hot(tp[d, pl.ds(groups + giver, 1), :])
            weights[d, 0:LANES, z * LANES : (z + 1) * LANES] = counts(put, given, KAPPA)
            weights[d, LANES : 2 * LANES, z * LANES : (z + 1) * LANES] = counts(
                asked, taken, 1.0
            )
        return 0

    lax.fori_loop(0, n_gx, build, 0)

    def p_copy(c, to, slot):
        return pltpu.make_async_remote_copy(
            src_ref=parts.at[lax.rem(c, 2), to], dst_ref=arrived.at[c, slot],
            send_sem=p_send.at[lax.rem(c, 2), to], recv_sem=p_recv.at[c, slot],
            device_id=(1 - sec, to, gy), device_id_type=MESH,
        )

    def second(c, _):
        others(lambda at: z_copy(c, at, at).wait_recv())
        for z in range(n_gy):
            for k in range(chunk):
                rest = gz[z, c * chunk + k]
                for piece in range(3):
                    cut = rest.astype(BF16)
                    pieces[piece, z * LANES : (z + 1) * LANES, k * LANES : (k + 1) * LANES] = cut
                    rest = rest - cut.astype(F32)

        def one(d):
            @pl.when(c >= 2)
            def _():
                p_copy(c, d, gx).wait_send()

            made = jnp.dot(weights[d], pieces[0], preferred_element_type=F32)
            made = made + jnp.dot(weights[d], pieces[1], preferred_element_type=F32)
            made = made + jnp.dot(weights[d], pieces[2], preferred_element_type=F32)
            for k in range(chunk):
                for h in range(2):
                    parts[lax.rem(c, 2), d, k, h] = made[
                        h * LANES : (h + 1) * LANES, k * LANES : (k + 1) * LANES
                    ]
            p_copy(c, d, gx).start()

        plane(one)
        return 0

    lax.fori_loop(0, chunks, second, 0)

    def third(c, _):
        plane(lambda at: p_copy(c, at, at).wait_recv())

        def one(k, _):
            def add(d, sums):
                return sums[0] + arrived[c, d, k, 0], sums[1] + arrived[c, d, k, 1]

            plain, scaled = lax.fori_loop(
                1, n_gx, add, (arrived[c, 0, k, 0], arrived[c, 0, k, 1])
            )
            old = gz[gy, c * chunk + k]
            xe[c * chunk + k, EDGE : EDGE + rows, 0:LANES] = (
                old + plain + jnp.tanh(old) * scaled
            )
            return 0

        lax.fori_loop(0, chunk, one, 0)
        return 0

    lax.fori_loop(0, chunks, third, 0)

    planes = [
        functools.partial(lambda l: xe[l, EDGE : EDGE + rows, 0:LANES], l)
        for l in range(levels)
    ]
    pack(planes, rs2, ps2)
    halo_start(1, rs2, rr2, ps2, pr2)
    halo_wait(1, rs2, rr2, ps2, pr2)
    for l in range(levels):
        xe[l, 0:EDGE, 0:LANES] = rr2[0, l]
        xe[l, EDGE + rows : tall, 0:LANES] = rr2[1, l]
        xe[l, :, LANES : 2 * LANES] = beside(pr2, l)

    def last(l, _):
        out_ref[0, l] = sweeps(l)
        return 0

    lax.fori_loop(0, levels, last, 0)

    others(lambda to: table_z(to, gy).wait_send())
    plane(lambda to: table_p(to, gx).wait_send())

    def drain(c, _):
        others(lambda to: z_copy(c, to, gy).wait_send())
        return 0

    lax.fori_loop(0, chunks, drain, 0)
    for c in range(max(0, chunks - 2), chunks):
        plane(lambda to: p_copy(c, to, gx).wait_send())


def body(n_gx, n_gy, adjoint_state, forcing, viscosity, reaction, source_patch, owner, cavity_map):
    levels, rows = adjoint_state.shape[1:3]
    groups, cap = cavity_map.shape[2:]
    chunk = 2 if levels % 2 == 0 else 1
    chunks = levels // chunk
    tall = rows + 2 * EDGE
    n1, n2 = 2 * levels + 1, levels
    k1, k2 = -(-n1 // 16), -(-n2 // 16)
    dma = pltpu.SemaphoreType.DMA
    vmem = pl.BlockSpec(memory_space=pltpu.VMEM)
    return pl.pallas_call(
        functools.partial(kernel, n_gx, n_gy, groups, cap, levels, chunk),
        out_shape=jax.ShapeDtypeStruct(adjoint_state.shape, F32),
        in_specs=[vmem] * 7,
        out_specs=vmem,
        scratch_shapes=[
            pltpu.VMEM((levels, tall, 2 * LANES), F32),
            pltpu.VMEM((levels, tall, 2 * LANES), F32),
            pltpu.VMEM((tall, 2 * LANES), F32),
            pltpu.VMEM((2, n1, EDGE, LANES), F32),
            pltpu.VMEM((2, n1, EDGE, LANES), F32),
            pltpu.VMEM((k1, rows, LANES), F32),
            pltpu.VMEM((2, k1, tall, LANES), F32),
            pltpu.VMEM((2, n2, EDGE, LANES), F32),
            pltpu.VMEM((2, n2, EDGE, LANES), F32),
            pltpu.VMEM((k2, rows, LANES), F32),
            pltpu.VMEM((2, k2, tall, LANES), F32),
            pltpu.VMEM((n_gy, 2 * groups, LANES), F32),
            pltpu.VMEM((n_gx, 2 * groups, LANES), F32),
            pltpu.VMEM((n_gx, 2 * LANES, n_gy * LANES), BF16),
            pltpu.VMEM((3, n_gy * LANES, chunk * LANES), BF16),
            pltpu.VMEM((n_gy, levels, rows, LANES), F32),
            pltpu.VMEM((2, n_gx, chunk, 2, rows, LANES), F32),
            pltpu.VMEM((chunks, n_gx, chunk, 2, rows, LANES), F32),
            dma((2, 8)), dma((2, 8)),
            dma((n_gy,)), dma((n_gy,)), dma((n_gx,)), dma((n_gx,)),
            dma((chunks, n_gy)), dma((chunks, n_gy)), dma((2, n_gx)), dma((chunks, n_gx)),
        ],
        compiler_params=pltpu.CompilerParams(
            collective_id=0, has_side_effects=True, vmem_limit_bytes=60 * 2**20
        ),
    )(adjoint_state, forcing, viscosity, reaction, source_patch, owner, cavity_map)


def solution(mesh):
    return jax.shard_map(
        functools.partial(body, mesh.shape["gx"], mesh.shape["gy"]),
        mesh=mesh,
        in_specs=(
            P("sec", None, "gx", "gy"),
            P("sec", None, "gx", "gy"),
            P("sec", "gx", "gy"),
            P("sec", "gx", "gy"),
            P("sec", ("gx", "gy")),
            P("sec", ("gx", "gy"), None),
            P("sec", ("gx", "gy"), None, None),
        ),
        out_specs=P("sec", None, "gx", "gy"),
        check_vma=False,
    )
```

```python
import functools

import jax
import jax.numpy as jnp
from jax import lax
from jax.experimental import pallas as pl
from jax.experimental.pallas import tpu as pltpu
from jax.sharding import PartitionSpec as P

OMEGA = 0.8
KAPPA = 0.5
HALF = 4
EDGE = 8
LANES = 128
MESH = pl.DeviceIdType.MESH
BF16 = jnp.bfloat16
F32 = jnp.float32


def iota(shape, dim):
    return lax.broadcasted_iota(jnp.int32, shape, dim)


def kernel(
    n_gx, n_gy, groups, cap, levels, chunk, square,
    x_ref, f_ref, v_ref, r_ref, src_ref, own_ref, map_ref, out_ref,
    xe, fe, be, rs1, rr1, ps1, pr1, rs2, rr2, ps2, pr2,
    tz, tp, weights, pieces, gz, parts, relay, arrived,
    halo_send, halo_recv, halo_send2, halo_recv2, tz_send, tz_recv, tp_send, tp_recv,
    z_send, z_recv, p_send, p_recv, r_send, r_recv,
):
    sec, gx, gy = lax.axis_index("sec"), lax.axis_index("gx"), lax.axis_index("gy")
    rows = x_ref.shape[2]
    tall = rows + 2 * EDGE
    chunks = levels // chunk
    has = {-1: gx > 0, 0: True, 1: gx < n_gx - 1}
    has_y = {-1: gy > 0, 0: True, 1: gy < n_gy - 1}
    around = [(a, b) for a in (-1, 0, 1) for b in (-1, 0, 1) if (a, b) != (0, 0)]

    def beyond(e):
        if not square:
            return lax.rem(gx + e, n_gx)
        if e == 0:
            return gx
        if e == 1:
            return gx + 1 - 2 * (gx % 2)
        if e == 2:
            return gx + 2 - 4 * (gx // 2)
        return n_gx - 1 - gx

    def exists(a, b):
        if a == 0:
            return has_y[b]
        if b == 0:
            return has[a]
        return jnp.logical_and(has[a], has_y[b])

    lane = iota((LANES, LANES), 1)
    row = iota((LANES, LANES), 0)
    named = jnp.where(own_ref[0] == lane, 1.0, 0.0).astype(BF16)
    earlier = jnp.where(lane < row, 1.0, 0.0).astype(BF16)
    before = jnp.dot(earlier, named, preferred_element_type=F32)
    rank = jnp.sum(before * named.astype(F32), axis=1, keepdims=True)
    source = jnp.sum(
        jnp.where(lane == row, src_ref[...].astype(F32) + 1.0, 0.0), axis=1, keepdims=True
    )
    ranked = jnp.where(rank == lane.astype(F32), source, 0.0).astype(BF16)
    slots = lax.dot_general(
        named, ranked, (((0,), (0,)), ((), ())), preferred_element_type=F32
    )
    tz[gy, 0:groups] = slots[0:groups]
    tz[gy, groups : 2 * groups] = jnp.full((groups, LANES), -1.0, F32)
    tz[gy, groups : 2 * groups, 0:cap] = map_ref[0, 0].astype(F32)

    inv = OMEGA / (4.0 * v_ref[0] + r_ref[0])
    be[...] = jnp.zeros_like(be)
    be[EDGE : EDGE + rows, 0:LANES] = inv * v_ref[0]
    for l in range(levels):
        fe[l, EDGE : EDGE + rows, 0:LANES] = inv * f_ref[0, l]

    def pack(planes, rs, ps):
        small = iota((rows, LANES), 1)
        for first in range(0, len(planes), 16):
            packed = jnp.zeros((rows, LANES), F32)
            for k, read in enumerate(planes[first : first + 16]):
                tile = read()
                rs[0, first + k] = tile[0:EDGE]
                rs[1, first + k] = tile[rows - EDGE : rows]
                low = tile if k == 0 else pltpu.roll(tile, 8 * k, 1)
                high = tile if k == 15 else pltpu.roll(tile, 8 * k + 8, 1)
                packed = jnp.where(small // 4 == 2 * k, low, packed)
                packed = jnp.where(small // 4 == 2 * k + 1, high, packed)
            ps[first // 16] = packed

    def halo_copy(a, b, rs, rr, ps, pr, ss, sr):
        if b == 0:
            src, dst = rs.at[(a + 1) // 2], rr.at[(1 - a) // 2]
        else:
            side = (1 - b) // 2
            if a == 0:
                src, dst = ps, pr.at[side, :, EDGE : EDGE + rows]
            elif a == 1:
                src, dst = ps.at[:, rows - EDGE : rows], pr.at[side, :, 0:EDGE]
            else:
                src, dst = ps.at[:, 0:EDGE], pr.at[side, :, EDGE + rows : tall]
        k = around.index((a, b))
        return pltpu.make_async_remote_copy(
            src_ref=src, dst_ref=dst,
            send_sem=ss.at[k], recv_sem=sr.at[k],
            device_id=(sec, gx + a, gy + b), device_id_type=MESH,
        )

    def halo_start(refs):
        for a, b in around:
            @pl.when(exists(a, b))
            def _():
                halo_copy(a, b, *refs).start()

    def halo_wait(refs):
        for a, b in around:
            @pl.when(exists(-a, -b))
            def _():
                halo_copy(a, b, *refs).wait_recv()

    def halo_sent(refs):
        for a, b in around:
            @pl.when(exists(a, b))
            def _():
                halo_copy(a, b, *refs).wait_send()

    halo1 = (rs1, rr1, ps1, pr1, halo_send, halo_recv)

    def halo2(c):
        return tuple(r.at[c] for r in (rs2, rr2, ps2, pr2, halo_send2, halo_recv2))

    def beside(pr, k):
        small = iota((tall, LANES), 1)
        at = 8 * (k % 16)
        right, left = pr[1, k // 16], pr[0, k // 16]
        right = right if at == 0 else pltpu.roll(right, LANES - at, 1)
        left = left if at == 120 else pltpu.roll(left, 120 - at, 1)
        return jnp.where(small < HALF, right, jnp.where(small >= LANES - HALF, left, 0.0))

    def sweeps(l):
        field, push, pull = xe[l], fe[l], be[...]
        for _ in range(HALF):
            near = pltpu.roll(field, 1, 0) + pltpu.roll(field, tall - 1, 0)
            near = near + pltpu.roll(field, 1, 1) + pltpu.roll(field, 2 * LANES - 1, 1)
            field = (1.0 - OMEGA) * field + push + pull * near
        return field[EDGE : EDGE + rows, 0:LANES]

    planes = [functools.partial(lambda l: x_ref[0, l], l) for l in range(levels)]
    planes += [
        functools.partial(lambda l: fe[l, EDGE : EDGE + rows, 0:LANES], l)
        for l in range(levels)
    ]
    planes += [lambda: be[EDGE : EDGE + rows, 0:LANES]]
    pack(planes, rs1, ps1)
    for ref in (rr1, pr1, rr2, pr2):
        ref[...] = jnp.zeros_like(ref)

    barrier = pltpu.get_barrier_semaphore()

    def hello(*device):
        pl.semaphore_signal(barrier, inc=1, device_id=device, device_id_type=MESH)

    total = n_gx + n_gy - 1
    for k in range(1, n_gy):
        hello(sec, gx, lax.rem(gy + k, n_gy))
    for k in range(n_gx):
        hello(1 - sec, lax.rem(gx + k, n_gx), gy)
    for a, b in around:
        if a != 0:
            there = exists(a, b)
            total = total + jnp.where(there, 1, 0)

            @pl.when(there)
            def _():
                hello(sec, gx + a, gy + b)

    if square:
        total = total + 2
        for e in (1, 2):
            hello(sec, beyond(e), gy)
    pl.semaphore_wait(barrier, total)

    halo_start(halo1)

    def table_z(to, slot):
        return pltpu.make_async_remote_copy(
            src_ref=tz.at[gy], dst_ref=tz.at[slot],
            send_sem=tz_send.at[to], recv_sem=tz_recv.at[slot],
            device_id=(sec, gx, to), device_id_type=MESH,
        )

    def table_p(to, slot):
        return pltpu.make_async_remote_copy(
            src_ref=tz.at[gy], dst_ref=tp.at[slot],
            send_sem=tp_send.at[to], recv_sem=tp_recv.at[slot],
            device_id=(1 - sec, to, gy), device_id_type=MESH,
        )

    def others(act):
        def one(k, _):
            act(lax.rem(gy + k, n_gy))
            return 0
        lax.fori_loop(1, n_gy, one, 0)

    def plane(act):
        def one(k, _):
            act(lax.rem(gx + k, n_gx))
            return 0
        lax.fori_loop(0, n_gx, one, 0)

    others(lambda to: table_z(to, gy).start())
    plane(lambda to: table_p(to, gx).start())

    halo_wait(halo1)
    for l in range(levels):
        for ref, k in ((xe, l), (fe, levels + l)):
            ref[l, 0:EDGE, 0:LANES] = rr1[0, k]
            ref[l, EDGE + rows : tall, 0:LANES] = rr1[1, k]
            ref[l, :, LANES : 2 * LANES] = beside(pr1, k)
        xe[l, EDGE : EDGE + rows, 0:LANES] = x_ref[0, l]
    be[0:EDGE, 0:LANES] = rr1[0, 2 * levels]
    be[EDGE + rows : tall, 0:LANES] = rr1[1, 2 * levels]
    be[:, LANES : 2 * LANES] = beside(pr1, 2 * levels)

    def z_copy(step, c, slot):
        return pltpu.make_async_remote_copy(
            src_ref=gz.at[slot, pl.ds(c * chunk, chunk)],
            dst_ref=gz.at[slot, pl.ds(c * chunk, chunk)],
            send_sem=z_send.at[(step + 1) // 2, c, slot], recv_sem=z_recv.at[c, slot],
            device_id=(sec, gx, gy + step), device_id_type=MESH,
        )

    def z_start(step, c, slot):
        @pl.when(has_y[step])
        def _():
            z_copy(step, c, slot).start()

    def first(c):
        def one(k, _):
            gz[gy, c * chunk + k] = sweeps(c * chunk + k)
            return 0
        lax.fori_loop(0, chunk, one, 0)
        z_start(1, c, gy)
        z_start(-1, c, gy)

    def onward(c, d):
        @pl.when(gy >= d)
        def _():
            z_copy(1, c, gy - d).wait_recv()
            z_start(1, c, gy - d)

        @pl.when(gy + d < n_gy)
        def _():
            z_copy(-1, c, gy + d).wait_recv()
            z_start(-1, c, gy + d)

    first(0)

    others(lambda at: table_z(at, at).wait_recv())
    plane(lambda at: table_p(at, at).wait_recv())
    patch_row = (row // 2).astype(F32)
    same = (row % 2) == (lane % 2)

    def hot(values):
        return jnp.where(values == patch_row, 1.0, 0.0).astype(BF16)

    def counts(a, b, scale):
        both = lax.dot_general(a, b, (((1,), (1,)), ((), ())), preferred_element_type=F32)
        return jnp.where(same, scale * both, 0.0).astype(BF16)

    def build(d, _):
        dest = d * n_gy + gy
        for z in range(n_gy):
            giver = gx * n_gy + z
            given = hot(tz[z, pl.ds(dest, 1), :] - 1.0)
            taken = hot(tz[z, pl.ds(groups + dest, 1), :])
            asked = hot(tp[d, pl.ds(giver, 1), :] - 1.0)
            put = hot(tp[d, pl.ds(groups + giver, 1), :])
            weights[d, 0:LANES, z * LANES : (z + 1) * LANES] = counts(put, given, KAPPA)
            weights[d, LANES : 2 * LANES, z * LANES : (z + 1) * LANES] = counts(
                asked, taken, 1.0
            )
        return 0

    lax.fori_loop(0, n_gx, build, 0)

    def part_slot(c):
        return c if square else lax.rem(c, 2)

    def whole(c, e):
        return pltpu.make_async_remote_copy(
            src_ref=parts.at[part_slot(c), e], dst_ref=arrived.at[c, e],
            send_sem=p_send.at[part_slot(c), e, 0], recv_sem=p_recv.at[c, e, 0],
            device_id=(1 - sec, beyond(e), gy), device_id_type=MESH,
        )

    def single(c, e, k):
        return pltpu.make_async_remote_copy(
            src_ref=parts.at[c, e, k], dst_ref=arrived.at[c, e, k],
            send_sem=p_send.at[c, e, k], recv_sem=p_recv.at[c, e, k],
            device_id=(1 - sec, beyond(e), gy), device_id_type=MESH,
        )

    def corner(c, k):
        return pltpu.make_async_remote_copy(
            src_ref=parts.at[c, 3, k], dst_ref=relay.at[c, k],
            send_sem=r_send.at[c, k], recv_sem=r_recv.at[c, k],
            device_id=(sec, beyond(1 + k), gy), device_id_type=MESH,
        )

    def second(c):
        for z in range(n_gy):
            for k in range(chunk):
                rest = gz[z, c * chunk + k]
                for piece in range(3):
                    cut = rest.astype(BF16)
                    pieces[piece, z * LANES : (z + 1) * LANES, k * LANES : (k + 1) * LANES] = cut
                    rest = rest - cut.astype(F32)

        def make(e):
            w = weights[beyond(e)]
            made = jnp.dot(w, pieces[0], preferred_element_type=F32)
            made = made + jnp.dot(w, pieces[1], preferred_element_type=F32)
            made = made + jnp.dot(w, pieces[2], preferred_element_type=F32)
            for k in range(chunk):
                for h in range(2):
                    parts[part_slot(c), e, k, h] = made[
                        h * LANES : (h + 1) * LANES, k * LANES : (k + 1) * LANES
                    ]

        if square:
            make(3)
            corner(c, 0).start()
            corner(c, 1).start()
            make(1)
            single(c, 1, 0).start()
            make(2)
            single(c, 2, 1).start()
            make(0)
            whole(c, 0).start()
        else:
            def one(e, _):
                @pl.when(c >= 2)
                def _():
                    whole(c, e).wait_send()
                make(e)
                whole(c, e).start()
                return 0
            lax.fori_loop(0, n_gx, one, 0)

    def combine(c):
        if square:
            for k in range(2):
                corner(c, k).wait_recv()
                for h in range(2):
                    parts[c, 2 - k, k, h] = parts[c, 2 - k, k, h] + relay[c, k, h]
                single(c, 2 - k, k).start()

    def third(c):
        if square:
            whole(c, 0).wait_recv()
            for e in (1, 2):
                for k in range(2):
                    single(c, e, k).wait_recv()
        else:
            def arrive(e, _):
                whole(c, e).wait_recv()
                return 0
            lax.fori_loop(0, n_gx, arrive, 0)
        count = 3 if square else n_gx
        planes = []
        for k in range(chunk):
            def add(e, sums):
                return sums[0] + arrived[c, e, k, 0], sums[1] + arrived[c, e, k, 1]

            plain, scaled = lax.fori_loop(
                1, count, add, (arrived[c, 0, k, 0], arrived[c, 0, k, 1])
            )
            old = gz[gy, c * chunk + k]
            new = old + plain + jnp.tanh(old) * scaled
            xe[c * chunk + k, EDGE : EDGE + rows, 0:LANES] = new
            planes.append(functools.partial(lambda new: new, new))
        pack(planes, rs2.at[c], ps2.at[c])
        halo_start(halo2(c))

    def last(c):
        halo_wait(halo2(c))
        for k in range(chunk):
            l = c * chunk + k
            xe[l, 0:EDGE, 0:LANES] = rr2[c, 0, k]
            xe[l, EDGE + rows : tall, 0:LANES] = rr2[c, 1, k]
            xe[l, :, LANES : 2 * LANES] = beside(pr2.at[c], k)

        def one(k, _):
            out_ref[0, c * chunk + k] = sweeps(c * chunk + k)
            return 0
        lax.fori_loop(0, chunk, one, 0)

    stages = [first] + [functools.partial(lambda d, c: onward(c, d), d) for d in range(1, n_gy)]
    lags = list(range(n_gy)) + [n_gy - 1, n_gy, n_gy + 1, n_gy + 2]
    stages += [second, combine, third, last]

    def turn(i, _):
        for lag, stage in zip(lags, stages):
            c = i - lag

            @pl.when(jnp.logical_and(c >= (1 if lag == 0 else 0), c < chunks))
            def _():
                stage(c)
        return 0

    lax.fori_loop(1, chunks + lags[-1], turn, 0)

    others(lambda to: table_z(to, gy).wait_send())
    plane(lambda to: table_p(to, gx).wait_send())
    halo_sent(halo1)

    def drain(c, _):
        halo_sent(halo2(c))

        def slot(z, _):
            @pl.when(jnp.logical_and(z <= gy, has_y[1]))
            def _():
                z_copy(1, c, z).wait_send()

            @pl.when(jnp.logical_and(z >= gy, has_y[-1]))
            def _():
                z_copy(-1, c, z).wait_send()
            return 0

        lax.fori_loop(0, n_gy, slot, 0)
        if square:
            whole(c, 0).wait_send()
            for k in range(2):
                corner(c, k).wait_send()
                for e in (1, 2):
                    single(c, e, k).wait_send()
        return 0

    lax.fori_loop(0, chunks, drain, 0)
    if not square:
        for c in range(max(0, chunks - 2), chunks):
            def left(e, _):
                whole(c, e).wait_send()
                return 0
            lax.fori_loop(0, n_gx, left, 0)


def body(n_gx, n_gy, adjoint_state, forcing, viscosity, reaction, source_patch, owner, cavity_map):
    levels, rows = adjoint_state.shape[1:3]
    groups, cap = cavity_map.shape[2:]
    chunk = 2 if levels % 2 == 0 else 1
    chunks = levels // chunk
    tall = rows + 2 * EDGE
    n1 = 2 * levels + 1
    k1 = -(-n1 // 16)
    square = n_gx == 4 and chunk == 2
    slots = chunks if square else 2
    roles = 3 if square else n_gx
    dma = pltpu.SemaphoreType.DMA
    vmem = pl.BlockSpec(memory_space=pltpu.VMEM)
    return pl.pallas_call(
        functools.partial(kernel, n_gx, n_gy, groups, cap, levels, chunk, square),
        out_shape=jax.ShapeDtypeStruct(adjoint_state.shape, F32),
        in_specs=[vmem] * 7,
        out_specs=vmem,
        scratch_shapes=[
            pltpu.VMEM((levels, tall, 2 * LANES), F32),
            pltpu.VMEM((levels, tall, 2 * LANES), F32),
            pltpu.VMEM((tall, 2 * LANES), F32),
            pltpu.VMEM((2, n1, EDGE, LANES), F32),
            pltpu.VMEM((2, n1, EDGE, LANES), F32),
            pltpu.VMEM((k1, rows, LANES), F32),
            pltpu.VMEM((2, k1, tall, LANES), F32),
            pltpu.VMEM((chunks, 2, chunk, EDGE, LANES), F32),
            pltpu.VMEM((chunks, 2, chunk, EDGE, LANES), F32),
            pltpu.VMEM((chunks, 1, rows, LANES), F32),
            pltpu.VMEM((chunks, 2, 1, tall, LANES), F32),
            pltpu.VMEM((n_gy, 2 * groups, LANES), F32),
            pltpu.VMEM((n_gx, 2 * groups, LANES), F32),
            pltpu.VMEM((n_gx, 2 * LANES, n_gy * LANES), BF16),
            pltpu.VMEM((3, n_gy * LANES, chunk * LANES), BF16),
            pltpu.VMEM((n_gy, levels, rows, LANES), F32),
            pltpu.VMEM((slots, n_gx, chunk, 2, rows, LANES), F32),
            pltpu.VMEM((chunks, 2, 2, rows, LANES) if square else (8, LANES), F32),
            pltpu.VMEM((chunks, roles, chunk, 2, rows, LANES), F32),
            dma((8,)), dma((8,)), dma((chunks, 8)), dma((chunks, 8)),
            dma((n_gy,)), dma((n_gy,)), dma((n_gx,)), dma((n_gx,)),
            dma((2, chunks, n_gy)), dma((chunks, n_gy)),
            dma((slots, n_gx, chunk)), dma((chunks, roles, chunk)),
            dma((chunks, 2)), dma((chunks, 2)),
        ],
        compiler_params=pltpu.CompilerParams(
            collective_id=0, has_side_effects=True, vmem_limit_bytes=60 * 2**20
        ),
    )(adjoint_state, forcing, viscosity, reaction, source_patch, owner, cavity_map)


def solution(mesh):
    return jax.shard_map(
        functools.partial(body, mesh.shape["gx"], mesh.shape["gy"]),
        mesh=mesh,
        in_specs=(
            P("sec", None, "gx", "gy"),
            P("sec", None, "gx", "gy"),
            P("sec", "gx", "gy"),
            P("sec", "gx", "gy"),
            P("sec", ("gx", "gy")),
            P("sec", ("gx", "gy"), None),
            P("sec", ("gx", "gy"), None, None),
        ),
        out_specs=P("sec", None, "gx", "gy"),
        check_vma=False,
    )
```

```python
import functools

import jax
import jax.numpy as jnp
from jax import lax
from jax.experimental import pallas as pl
from jax.experimental.pallas import tpu as pltpu
from jax.sharding import PartitionSpec as P

OMEGA = 0.8
KAPPA = 0.5
HALF = 4
EDGE = 8
LANES = 128
MESH = pl.DeviceIdType.MESH
BF16 = jnp.bfloat16
F32 = jnp.float32


def iota(shape, dim):
    return lax.broadcasted_iota(jnp.int32, shape, dim)


def kernel(
    n_gx, n_gy, groups, cap, levels, chunk, square,
    x_ref, f_ref, v_ref, r_ref, src_ref, own_ref, map_ref, out_ref,
    xe, fe, be, rs1, rr1, ps1, pr1, rs2, rr2, ps2, pr2,
    tz, tp, weights, pieces, gz, parts, relay, arrived,
    halo_send, halo_recv, halo_send2, halo_recv2, tz_send, tz_recv, tp_send, tp_recv,
    z_send, z_recv, p_send, p_recv, r_send, r_recv,
):
    sec, gx, gy = lax.axis_index("sec"), lax.axis_index("gx"), lax.axis_index("gy")
    rows = x_ref.shape[2]
    tall = rows + 2 * EDGE
    chunks = levels // chunk
    has = {-1: gx > 0, 0: True, 1: gx < n_gx - 1}
    has_y = {-1: gy > 0, 0: True, 1: gy < n_gy - 1}
    around = [(a, b) for a in (-1, 0, 1) for b in (-1, 0, 1) if (a, b) != (0, 0)]

    def beyond(e):
        if not square:
            return lax.rem(gx + e, n_gx)
        if e == 0:
            return gx
        if e == 1:
            return gx + 1 - 2 * (gx % 2)
        if e == 2:
            return gx + 2 - 4 * (gx // 2)
        return n_gx - 1 - gx

    def exists(a, b):
        if a == 0:
            return has_y[b]
        if b == 0:
            return has[a]
        return jnp.logical_and(has[a], has_y[b])

    lane = iota((LANES, LANES), 1)
    row = iota((LANES, LANES), 0)
    owner = jnp.sum(
        jnp.where(lane == row, own_ref[...].astype(F32), 0.0), axis=1, keepdims=True
    )
    named = jnp.where(owner == lane.astype(F32), 1.0, 0.0).astype(BF16)
    earlier = jnp.where(lane < row, 1.0, 0.0).astype(BF16)
    before = jnp.dot(earlier, named, preferred_element_type=F32)
    rank = jnp.sum(before * named.astype(F32), axis=1, keepdims=True)
    source = jnp.sum(
        jnp.where(lane == row, src_ref[...].astype(F32) + 1.0, 0.0), axis=1, keepdims=True
    )
    ranked = jnp.where(rank == lane.astype(F32), source, 0.0).astype(BF16)
    slots = lax.dot_general(
        named, ranked, (((0,), (0,)), ((), ())), preferred_element_type=F32
    )
    tz[gy, 0:groups] = slots[0:groups]
    tz[gy, groups : 2 * groups] = jnp.full((groups, LANES), -1.0, F32)
    tz[gy, groups : 2 * groups, 0:cap] = map_ref[0, 0].astype(F32)

    inv = OMEGA / (4.0 * v_ref[0] + r_ref[0])
    be[...] = jnp.zeros_like(be)
    be[EDGE : EDGE + rows, 0:LANES] = inv * v_ref[0]
    for l in range(levels):
        fe[l, EDGE : EDGE + rows, 0:LANES] = inv * f_ref[0, l]

    def pack(planes, rs, ps):
        small = iota((rows, LANES), 1)
        for first in range(0, len(planes), 16):
            packed = jnp.zeros((rows, LANES), F32)
            for k, read in enumerate(planes[first : first + 16]):
                tile = read()
                rs[0, first + k] = tile[0:EDGE]
                rs[1, first + k] = tile[rows - EDGE : rows]
                low = tile if k == 0 else pltpu.roll(tile, 8 * k, 1)
                high = tile if k == 15 else pltpu.roll(tile, 8 * k + 8, 1)
                packed = jnp.where(small // 4 == 2 * k, low, packed)
                packed = jnp.where(small // 4 == 2 * k + 1, high, packed)
            ps[first // 16] = packed

    def halo_copy(a, b, rs, rr, ps, pr, ss, sr):
        if b == 0:
            src, dst = rs.at[(a + 1) // 2], rr.at[(1 - a) // 2]
        else:
            side = (1 - b) // 2
            if a == 0:
                src, dst = ps, pr.at[side, :, EDGE : EDGE + rows]
            elif a == 1:
                src, dst = ps.at[:, rows - EDGE : rows], pr.at[side, :, 0:EDGE]
            else:
                src, dst = ps.at[:, 0:EDGE], pr.at[side, :, EDGE + rows : tall]
        k = around.index((a, b))
        return pltpu.make_async_remote_copy(
            src_ref=src, dst_ref=dst,
            send_sem=ss.at[k], recv_sem=sr.at[k],
            device_id=(sec, gx + a, gy + b), device_id_type=MESH,
        )

    def halo_start(refs):
        for a, b in around:
            @pl.when(exists(a, b))
            def _():
                halo_copy(a, b, *refs).start()

    def halo_wait(refs):
        for a, b in around:
            @pl.when(exists(-a, -b))
            def _():
                halo_copy(a, b, *refs).wait_recv()

    def halo_sent(refs):
        for a, b in around:
            @pl.when(exists(a, b))
            def _():
                halo_copy(a, b, *refs).wait_send()

    halo1 = (rs1, rr1, ps1, pr1, halo_send, halo_recv)

    def halo2(c):
        return tuple(r.at[c] for r in (rs2, rr2, ps2, pr2, halo_send2, halo_recv2))

    def beside(pr, k):
        small = iota((tall, LANES), 1)
        at = 8 * (k % 16)
        right, left = pr[1, k // 16], pr[0, k // 16]
        right = right if at == 0 else pltpu.roll(right, LANES - at, 1)
        left = left if at == 120 else pltpu.roll(left, 120 - at, 1)
        return jnp.where(small < HALF, right, jnp.where(small >= LANES - HALF, left, 0.0))

    def sweeps(l):
        field, push, pull = xe[l], fe[l], be[...]
        for _ in range(HALF):
            near = pltpu.roll(field, 1, 0) + pltpu.roll(field, tall - 1, 0)
            near = near + pltpu.roll(field, 1, 1) + pltpu.roll(field, 2 * LANES - 1, 1)
            field = (1.0 - OMEGA) * field + push + pull * near
        return field[EDGE : EDGE + rows, 0:LANES]

    planes = [functools.partial(lambda l: x_ref[0, l], l) for l in range(levels)]
    planes += [
        functools.partial(lambda l: fe[l, EDGE : EDGE + rows, 0:LANES], l)
        for l in range(levels)
    ]
    planes += [lambda: be[EDGE : EDGE + rows, 0:LANES]]
    pack(planes, rs1, ps1)
    for ref in (rr1, pr1, rr2, pr2):
        ref[...] = jnp.zeros_like(ref)

    barrier = pltpu.get_barrier_semaphore()

    def hello(*device):
        pl.semaphore_signal(barrier, inc=1, device_id=device, device_id_type=MESH)

    total = n_gx + n_gy - 1
    for k in range(1, n_gy):
        hello(sec, gx, lax.rem(gy + k, n_gy))
    for k in range(n_gx):
        hello(1 - sec, lax.rem(gx + k, n_gx), gy)
    for a, b in around:
        if a != 0:
            there = exists(a, b)
            total = total + jnp.where(there, 1, 0)

            @pl.when(there)
            def _():
                hello(sec, gx + a, gy + b)

    if square:
        total = total + 2
        for e in (1, 2):
            hello(sec, beyond(e), gy)
    pl.semaphore_wait(barrier, total)

    halo_start(halo1)

    def table_z(to, slot):
        return pltpu.make_async_remote_copy(
            src_ref=tz.at[gy], dst_ref=tz.at[slot],
            send_sem=tz_send.at[to], recv_sem=tz_recv.at[slot],
            device_id=(sec, gx, to), device_id_type=MESH,
        )

    def table_p(to, slot):
        return pltpu.make_async_remote_copy(
            src_ref=tz.at[gy], dst_ref=tp.at[slot],
            send_sem=tp_send.at[to], recv_sem=tp_recv.at[slot],
            device_id=(1 - sec, to, gy), device_id_type=MESH,
        )

    def others(act):
        def one(k, _):
            act(lax.rem(gy + k, n_gy))
            return 0
        lax.fori_loop(1, n_gy, one, 0)

    def plane(act):
        def one(k, _):
            act(lax.rem(gx + k, n_gx))
            return 0
        lax.fori_loop(0, n_gx, one, 0)

    others(lambda to: table_z(to, gy).start())
    plane(lambda to: table_p(to, gx).start())

    halo_wait(halo1)
    for l in range(levels):
        for ref, k in ((xe, l), (fe, levels + l)):
            ref[l, 0:EDGE, 0:LANES] = rr1[0, k]
            ref[l, EDGE + rows : tall, 0:LANES] = rr1[1, k]
            ref[l, :, LANES : 2 * LANES] = beside(pr1, k)
        xe[l, EDGE : EDGE + rows, 0:LANES] = x_ref[0, l]
    be[0:EDGE, 0:LANES] = rr1[0, 2 * levels]
    be[EDGE + rows : tall, 0:LANES] = rr1[1, 2 * levels]
    be[:, LANES : 2 * LANES] = beside(pr1, 2 * levels)

    def z_copy(step, c, slot):
        return pltpu.make_async_remote_copy(
            src_ref=gz.at[slot, pl.ds(c * chunk, chunk)],
            dst_ref=gz.at[slot, pl.ds(c * chunk, chunk)],
            send_sem=z_send.at[(step + 1) // 2, c, slot], recv_sem=z_recv.at[c, slot],
            device_id=(sec, gx, gy + step), device_id_type=MESH,
        )

    def z_start(step, c, slot):
        @pl.when(has_y[step])
        def _():
            z_copy(step, c, slot).start()

    def first(c):
        def one(k, _):
            gz[gy, c * chunk + k] = sweeps(c * chunk + k)
            return 0
        lax.fori_loop(0, chunk, one, 0)
        z_start(1, c, gy)
        z_start(-1, c, gy)

    def onward(c, d):
        @pl.when(gy >= d)
        def _():
            z_copy(1, c, gy - d).wait_recv()
            z_start(1, c, gy - d)

        @pl.when(gy + d < n_gy)
        def _():
            z_copy(-1, c, gy + d).wait_recv()
            z_start(-1, c, gy + d)

    first(0)

    others(lambda at: table_z(at, at).wait_recv())
    plane(lambda at: table_p(at, at).wait_recv())
    patch_row = (row // 2).astype(F32)
    same = (row % 2) == (lane % 2)

    def hot(values):
        return jnp.where(values == patch_row, 1.0, 0.0).astype(BF16)

    def counts(a, b, scale):
        both = lax.dot_general(a, b, (((1,), (1,)), ((), ())), preferred_element_type=F32)
        return jnp.where(same, scale * both, 0.0).astype(BF16)

    def build(d, _):
        dest = d * n_gy + gy
        for z in range(n_gy):
            giver = gx * n_gy + z
            given = hot(tz[z, pl.ds(dest, 1), :] - 1.0)
            taken = hot(tz[z, pl.ds(groups + dest, 1), :])
            asked = hot(tp[d, pl.ds(giver, 1), :] - 1.0)
            put = hot(tp[d, pl.ds(groups + giver, 1), :])
            weights[d, 0:LANES, z * LANES : (z + 1) * LANES] = counts(put, given, KAPPA)
            weights[d, LANES : 2 * LANES, z * LANES : (z + 1) * LANES] = counts(
                asked, taken, 1.0
            )
        return 0

    lax.fori_loop(0, n_gx, build, 0)

    def part_slot(c):
        return c if square else lax.rem(c, 2)

    def whole(c, e):
        return pltpu.make_async_remote_copy(
            src_ref=parts.at[part_slot(c), e], dst_ref=arrived.at[c, e],
            send_sem=p_send.at[part_slot(c), e, 0], recv_sem=p_recv.at[c, e, 0],
            device_id=(1 - sec, beyond(e), gy), device_id_type=MESH,
        )

    def single(c, e, k):
        return pltpu.make_async_remote_copy(
            src_ref=parts.at[c, e, k], dst_ref=arrived.at[c, e, k],
            send_sem=p_send.at[c, e, k], recv_sem=p_recv.at[c, e, k],
            device_id=(1 - sec, beyond(e), gy), device_id_type=MESH,
        )

    def corner(c, k):
        return pltpu.make_async_remote_copy(
            src_ref=parts.at[c, 3, k], dst_ref=relay.at[c, k],
            send_sem=r_send.at[c, k], recv_sem=r_recv.at[c, k],
            device_id=(sec, beyond(1 + k), gy), device_id_type=MESH,
        )

    def second(c):
        for z in range(n_gy):
            for k in range(chunk):
                rest = gz[z, c * chunk + k]
                for piece in range(3):
                    cut = rest.astype(BF16)
                    pieces[piece, z * LANES : (z + 1) * LANES, k * LANES : (k + 1) * LANES] = cut
                    rest = rest - cut.astype(F32)

        def make(e):
            w = weights[beyond(e)]
            made = jnp.dot(w, pieces[0], preferred_element_type=F32)
            made = made + jnp.dot(w, pieces[1], preferred_element_type=F32)
            made = made + jnp.dot(w, pieces[2], preferred_element_type=F32)
            for k in range(chunk):
                for h in range(2):
                    parts[part_slot(c), e, k, h] = made[
                        h * LANES : (h + 1) * LANES, k * LANES : (k + 1) * LANES
                    ]

        if square:
            make(3)
            corner(c, 0).start()
            corner(c, 1).start()
            make(1)
            single(c, 1, 0).start()
            make(2)
            single(c, 2, 1).start()
            make(0)
            whole(c, 0).start()
        else:
            def one(e, _):
                @pl.when(c >= 2)
                def _():
                    whole(c, e).wait_send()
                make(e)
                whole(c, e).start()
                return 0
            lax.fori_loop(0, n_gx, one, 0)

    def combine(c):
        if square:
            for k in range(2):
                corner(c, k).wait_recv()
                for h in range(2):
                    parts[c, 2 - k, k, h] = parts[c, 2 - k, k, h] + relay[c, k, h]
                single(c, 2 - k, k).start()

    def third(c):
        if square:
            whole(c, 0).wait_recv()
            for e in (1, 2):
                for k in range(2):
                    single(c, e, k).wait_recv()
        else:
            def arrive(e, _):
                whole(c, e).wait_recv()
                return 0
            lax.fori_loop(0, n_gx, arrive, 0)
        count = 3 if square else n_gx
        planes = []
        for k in range(chunk):
            def add(e, sums):
                return sums[0] + arrived[c, e, k, 0], sums[1] + arrived[c, e, k, 1]

            plain, scaled = lax.fori_loop(
                1, count, add, (arrived[c, 0, k, 0], arrived[c, 0, k, 1])
            )
            old = gz[gy, c * chunk + k]
            new = old + plain + jnp.tanh(old) * scaled
            xe[c * chunk + k, EDGE : EDGE + rows, 0:LANES] = new
            planes.append(functools.partial(lambda new: new, new))
        pack(planes, rs2.at[c], ps2.at[c])
        halo_start(halo2(c))

    def last(c):
        halo_wait(halo2(c))
        for k in range(chunk):
            l = c * chunk + k
            xe[l, 0:EDGE, 0:LANES] = rr2[c, 0, k]
            xe[l, EDGE + rows : tall, 0:LANES] = rr2[c, 1, k]
            xe[l, :, LANES : 2 * LANES] = beside(pr2.at[c], k)

        def one(k, _):
            out_ref[0, c * chunk + k] = sweeps(c * chunk + k)
            return 0
        lax.fori_loop(0, chunk, one, 0)

    stages = [first] + [functools.partial(lambda d, c: onward(c, d), d) for d in range(1, n_gy)]
    lags = list(range(n_gy)) + [n_gy - 1, n_gy, n_gy + 1, n_gy + 2]
    stages += [second, combine, third, last]

    def turn(i, _):
        for lag, stage in zip(lags, stages):
            c = i - lag

            @pl.when(jnp.logical_and(c >= (1 if lag == 0 else 0), c < chunks))
            def _():
                stage(c)
        return 0

    lax.fori_loop(1, chunks + lags[-1], turn, 0)

    others(lambda to: table_z(to, gy).wait_send())
    plane(lambda to: table_p(to, gx).wait_send())
    halo_sent(halo1)

    def drain(c, _):
        halo_sent(halo2(c))

        def slot(z, _):
            @pl.when(jnp.logical_and(z <= gy, has_y[1]))
            def _():
                z_copy(1, c, z).wait_send()

            @pl.when(jnp.logical_and(z >= gy, has_y[-1]))
            def _():
                z_copy(-1, c, z).wait_send()
            return 0

        lax.fori_loop(0, n_gy, slot, 0)
        if square:
            whole(c, 0).wait_send()
            for k in range(2):
                corner(c, k).wait_send()
                for e in (1, 2):
                    single(c, e, k).wait_send()
        return 0

    lax.fori_loop(0, chunks, drain, 0)
    if not square:
        for c in range(max(0, chunks - 2), chunks):
            def left(e, _):
                whole(c, e).wait_send()
                return 0
            lax.fori_loop(0, n_gx, left, 0)


def body(n_gx, n_gy, adjoint_state, forcing, viscosity, reaction, source_patch, owner, cavity_map):
    levels, rows = adjoint_state.shape[1:3]
    groups, cap = cavity_map.shape[2:]
    chunk = 2 if levels % 2 == 0 else 1
    chunks = levels // chunk
    tall = rows + 2 * EDGE
    n1 = 2 * levels + 1
    k1 = -(-n1 // 16)
    square = n_gx == 4 and chunk == 2
    slots = chunks if square else 2
    roles = 3 if square else n_gx
    dma = pltpu.SemaphoreType.DMA
    vmem = pl.BlockSpec(memory_space=pltpu.VMEM)
    return pl.pallas_call(
        functools.partial(kernel, n_gx, n_gy, groups, cap, levels, chunk, square),
        out_shape=jax.ShapeDtypeStruct(adjoint_state.shape, F32),
        in_specs=[vmem] * 7,
        out_specs=vmem,
        scratch_shapes=[
            pltpu.VMEM((levels, tall, 2 * LANES), F32),
            pltpu.VMEM((levels, tall, 2 * LANES), F32),
            pltpu.VMEM((tall, 2 * LANES), F32),
            pltpu.VMEM((2, n1, EDGE, LANES), F32),
            pltpu.VMEM((2, n1, EDGE, LANES), F32),
            pltpu.VMEM((k1, rows, LANES), F32),
            pltpu.VMEM((2, k1, tall, LANES), F32),
            pltpu.VMEM((chunks, 2, chunk, EDGE, LANES), F32),
            pltpu.VMEM((chunks, 2, chunk, EDGE, LANES), F32),
            pltpu.VMEM((chunks, 1, rows, LANES), F32),
            pltpu.VMEM((chunks, 2, 1, tall, LANES), F32),
            pltpu.VMEM((n_gy, 2 * groups, LANES), F32),
            pltpu.VMEM((n_gx, 2 * groups, LANES), F32),
            pltpu.VMEM((n_gx, 2 * LANES, n_gy * LANES), BF16),
            pltpu.VMEM((3, n_gy * LANES, chunk * LANES), BF16),
            pltpu.VMEM((n_gy, levels, rows, LANES), F32),
            pltpu.VMEM((slots, n_gx, chunk, 2, rows, LANES), F32),
            pltpu.VMEM((chunks, 2, 2, rows, LANES) if square else (8, LANES), F32),
            pltpu.VMEM((chunks, roles, chunk, 2, rows, LANES), F32),
            dma((8,)), dma((8,)), dma((chunks, 8)), dma((chunks, 8)),
            dma((n_gy,)), dma((n_gy,)), dma((n_gx,)), dma((n_gx,)),
            dma((2, chunks, n_gy)), dma((chunks, n_gy)),
            dma((slots, n_gx, chunk)), dma((chunks, roles, chunk)),
            dma((chunks, 2)), dma((chunks, 2)),
        ],
        compiler_params=pltpu.CompilerParams(
            collective_id=0, has_side_effects=True, vmem_limit_bytes=60 * 2**20
        ),
    )(adjoint_state, forcing, viscosity, reaction, source_patch, owner[:, :, 0], cavity_map)


def solution(mesh):
    return jax.shard_map(
        functools.partial(body, mesh.shape["gx"], mesh.shape["gy"]),
        mesh=mesh,
        in_specs=(
            P("sec", None, "gx", "gy"),
            P("sec", None, "gx", "gy"),
            P("sec", "gx", "gy"),
            P("sec", "gx", "gy"),
            P("sec", ("gx", "gy")),
            P("sec", ("gx", "gy"), None),
            P("sec", ("gx", "gy"), None, None),
        ),
        out_specs=P("sec", None, "gx", "gy"),
        check_vma=False,
    )
```
